32 devices in a mesh: row: 8 (over y, x, core), col: 4 (over z).
Axes of the slice: x: 2, y: 2, z: 4, core: 2. Of those that a mesh axis runs over, the one named last changes fastest.
Arguments:
- features: bfloat16 [16384, 512], P(('col', 'row')), may hold values from -6 to 6
- tile_values: bfloat16 [8, 4, 6, 256, 256], P('row', 'col'), may hold values from -0.21875 to 0.21875
- tile_index: int32 [8, 4, 6], P('row', 'col'), may hold values from 0 to 127, as said below
- tile_count: int32 [8, 4], P('row', 'col'), may hold values from 1 to 6, as said below
- weight: bfloat16 [512, 512], replicated, may hold values from -0.25 to 0.25
- cotangent: bfloat16 [16384, 512], P(('row', 'col')), may hold values from -6 to 6
Outputs:
- output: bfloat16 [16384, 512], P(('row', 'col'))
- weight_grad: float32 [512, 512], replicated
The draws below stay inside these ranges and needn't reach their ends.
Inputs may be any that keep to these rules, and one draw needn't show every extreme that they name: `tile_index`: on each device the 6 slots hold different tile numbers. `tile_count`: some device has all 6 slots live.
All inputs are finite; a program needn't handle non-finite values.
Results may differ from the reference program's by a relative error of at most 0.024.
Values may be sent and summed in bfloat16 or wider, within the bound.
No kernel may reach another device: no remote copies, remote signals or barrier semaphores. Data moves between devices by JAX's collectives and lax.ppermute only.
A program may use at most 64 MiB of HBM per device.

```python
import math
import jax
import jax.numpy as jnp
from jax import lax

F = 512
BLK = 256
RBG = 8
KMAX = 6
CBG = 16
V = 16384
N_ROW = 8
N_COL = 4


def draw_tile_index(key, part):
    subkeys = jax.random.split(jax.random.fold_in(key, 11), N_ROW * N_COL)

    def one_device(subkey):
        return jax.random.permutation(subkey, RBG * CBG)[:KMAX]
    return jax.vmap(one_device)(subkeys).reshape(N_ROW, N_COL, KMAX).astype(jnp.int32)


def draw_tile_count(key, part):
    first = jax.random.randint(jax.random.fold_in(key, 21), (N_ROW, N_COL), 1, KMAX + 1)
    second = jax.random.randint(jax.random.fold_in(key, 22), (N_ROW, N_COL), 1, KMAX + 1)
    counts = jnp.minimum(first, second)
    chosen = jax.random.randint(jax.random.fold_in(key, 23), (), 0, N_ROW * N_COL)
    flat_ids = jnp.arange(N_ROW * N_COL).reshape(N_ROW, N_COL)
    return jnp.where(flat_ids == chosen, KMAX, counts).astype(jnp.int32)


def levels(key, extent, cuts, smallest, top_value):
    loudness, own = 1.0, jax.random.fold_in(key, 6)
    for position, parts in cuts:
        heights = jnp.exp(jax.random.uniform(jax.random.fold_in(own, position), (parts,), jnp.float32, smallest / len(cuts), top_value / len(cuts)))
        loudness = loudness * jnp.repeat(heights, extent[position] // parts).reshape([-1 if axis == position else 1 for axis in range(len(extent))])
    return loudness


def scatter_about(stream_key, extent, spread, bound, pieces=(), kind=jnp.bfloat16):
    array = spread * jax.random.normal(stream_key, extent, jnp.float32)
    if pieces:
        array = array * levels(stream_key, extent, pieces, -0.22, 0.18)
    return jnp.clip(array, -bound, bound).astype(kind)


def setup_inputs(seed: int = 0) -> dict:
    keys = jax.random.split(jax.random.key(seed), 7)
    features = scatter_about(keys[0], (V, F), 1.0, 6.0, ((0, 32),))
    tile_values = scatter_about(keys[1], (N_ROW, N_COL, KMAX, BLK, BLK), (BLK * KMAX * N_ROW // CBG) ** -0.5, 0.21875, ((0, 8), (1, 4)))
    tile_index = draw_tile_index(jax.random.fold_in(keys[6], 71), 0)
    tile_count = draw_tile_count(jax.random.fold_in(keys[6], 71), 0)
    weight = scatter_about(keys[4], (F, F), F ** -0.5, 0.25)
    cotangent = scatter_about(keys[5], (V, F), 1.0, 6.0, ((0, 32),))
    return {"features": features, "tile_values": tile_values, "tile_index": tile_index, "tile_count": tile_count, "weight": weight, "cotangent": cotangent}


def reference(features, tile_values, tile_index, tile_count, weight, cotangent):
    blocks = features.reshape(-1, BLK, F)

    def one_group(group):
        tile_vals = tile_values[group].astype(jnp.float32)
        tile_ids = tile_index[group]
        live_count = tile_count[group]
        row_slot = tile_ids // CBG
        col_slot = tile_ids % CBG
        global_col = jnp.arange(N_COL, dtype=jnp.int32)[:, None] * CBG + col_slot
        picked = blocks[global_col].astype(jnp.float32)
        is_live = jnp.arange(KMAX, dtype=jnp.int32)[None, :] < live_count[:, None]
        placing = ((row_slot[:, :, None] == jnp.arange(RBG, dtype=jnp.int32)[None, None, :]) & is_live[:, :, None]).astype(jnp.float32)
        products = jnp.einsum('ckab,ckbf->ckaf', tile_vals, picked)
        partial_value = jnp.einsum('ckr,ckaf->craf', placing, products).astype(jnp.bfloat16)
        partial_value = lax.optimization_barrier(partial_value)
        return lax.optimization_barrier(jnp.sum(partial_value.astype(jnp.float32), axis=0))
    summed = lax.map(one_group, jnp.arange(N_ROW, dtype=jnp.int32))
    aggregated = summed.reshape(-1, F).astype(jnp.bfloat16)
    preact = jnp.dot(aggregated, weight, preferred_element_type=jnp.float32)
    output = jnp.where(preact > 0, preact, jnp.expm1(jnp.minimum(preact, 0.0))).astype(jnp.bfloat16)
    slope = jnp.where(preact > 0, 1.0, jnp.exp(jnp.minimum(preact, 0.0)))
    grad_pre = (cotangent.astype(jnp.float32) * slope).astype(jnp.bfloat16)
    weight_grad = jnp.dot(aggregated.T, grad_pre, preferred_element_type=jnp.float32) * (1.0 / math.sqrt(V))
    return (output, weight_grad)
```

```python
import functools
import math

import jax
import jax.numpy as jnp
from jax import lax
from jax.experimental import pallas as pl
from jax.experimental.pallas import tpu as pltpu
from jax.sharding import PartitionSpec as P

BLK = 256
RBG = 8
CHUNKS = (256, 256)
VMEM_LIMIT = 48 * 1024 * 1024
F32, BF16 = jnp.float32, jnp.bfloat16


def swap(x, axis, mask):
    return lax.ppermute(x, axis, [(i, i ^ mask) for i in range(lax.axis_size(axis))])


def bit_reversed(i, bits):
    out = 0 * i
    for b in range(bits):
        out = out + (((i >> b) & 1) << (bits - 1 - b))
    return out


def gather_row(x):
    n = lax.axis_size("row")
    half = x.shape[0] // 2
    got = {0: x}
    for k in sorted(range(2, n, 2), key=lambda k: (bin(k).count("1"), k)):
        low, high = k & -k, 1 << (k.bit_length() - 1)
        if low == high:
            got[k] = swap(x, "row", k)
        else:
            top = swap(got[k ^ high][:half], "row", high)
            bottom = swap(got[k ^ low][half:], "row", low)
            got[k] = jnp.concatenate([top, bottom])
    for k in range(0, n, 2):
        got[k + 1] = swap(got[k], "row", 1)
    return [got[k] for k in range(n)]


def tiles_kernel(me_ref, index_ref, count_ref, tiles_ref, *refs, n_row, n_col):
    pieces, (low_ref, high_ref, picked, total) = refs[:n_row], refs[n_row:]
    kmax = tiles_ref.shape[0]
    rows = pieces[0].shape[0]
    part = min(BLK, rows)
    own = RBG * BLK // n_col
    step = min(BLK, own)
    bits = n_col.bit_length() - 1
    col_groups = rows * n_row // BLK
    me_row, me_col = me_ref[0], me_ref[1]
    total[...] = jnp.zeros_like(total)
    for k in range(kmax):
        number = index_ref[k]
        row_slot, col_slot = number // col_groups, number % col_groups
        live = k < count_ref[0]

        @pl.when(live)
        def _(k=k, row_slot=row_slot, col_slot=col_slot):
            for j in range(BLK // part):
                first = col_slot * BLK + j * part
                owner = (first // rows) ^ me_row
                offset = pl.multiple_of(first % rows, part)
                for p in range(n_row):
                    @pl.when(owner == p)
                    def _(p=p):
                        picked[j * part:(j + 1) * part, :] = pieces[p][pl.ds(offset, part), :]
            product = jnp.dot(tiles_ref[k], picked[...], preferred_element_type=F32)
            for j in range(BLK // step):
                first = row_slot * BLK + j * step
                place = bit_reversed((first // own) ^ me_col, bits) * own + first % own
                place = pl.ds(pl.multiple_of(place, step), step)
                total[place, :] += product[j * step:(j + 1) * step, :]
    middle = total.shape[0] // 2
    low_ref[...] = total[:middle, :].astype(BF16)
    high_ref[...] = total[middle:, :].astype(BF16)


def tile_products(me, index, count, tiles, pieces):
    n_row, n_col = lax.axis_size("row"), lax.axis_size("col")
    wide = pieces[0].shape[1]
    half = jax.ShapeDtypeStruct((RBG * BLK // 2, wide), BF16)
    smem, vmem = pl.BlockSpec(memory_space=pltpu.SMEM), pl.BlockSpec(memory_space=pltpu.VMEM)
    return pl.pallas_call(
        functools.partial(tiles_kernel, n_row=n_row, n_col=n_col),
        out_shape=(half, half),
        in_specs=[smem] * 3 + [vmem] * (1 + n_row),
        out_specs=(vmem, vmem),
        scratch_shapes=[pltpu.VMEM((BLK, wide), BF16), pltpu.VMEM((RBG * BLK, wide), F32)],
        compiler_params=pltpu.CompilerParams(vmem_limit_bytes=VMEM_LIMIT),
        cost_estimate=pl.CostEstimate(
            flops=2 * tiles.shape[0] * BLK * BLK * wide, bytes_accessed=6 * 1024 * 1024, transcendentals=0),
    )(me, index, count, tiles, *pieces)


def vertex_kernel(me_ref, weight_ref, cot_ref, *refs, n_row, n_chunk, scale):
    sums, (out_ref, keep_ref, send_ref, agg, grad) = refs[:3 * n_chunk], refs[3 * n_chunk:]
    me_row = me_ref[0]
    at = 0
    for j in range(n_chunk):
        a, b, c = sums[3 * j:3 * j + 3]
        wide = a.shape[1]
        agg[:, at:at + wide] = (a[...].astype(F32) + b[...].astype(F32) + c[...].astype(F32)).astype(BF16)
        at += wide
    aggregated = agg[...]
    preact = jnp.dot(aggregated, weight_ref[...], preferred_element_type=F32)
    power = jnp.exp(jnp.minimum(preact, 0.0))
    positive = preact > 0
    out_ref[...] = jnp.where(positive, preact, power - 1.0).astype(BF16)
    grad_pre = (cot_ref[...].astype(F32) * jnp.where(positive, 1.0, power)).astype(BF16)
    grad[...] = lax.dot_general(aggregated, grad_pre, (((0,), (0,)), ((), ())), preferred_element_type=F32) * scale
    part = grad.shape[0] // n_row
    for k in range(n_row):
        rows = grad[pl.ds(pl.multiple_of((me_row ^ k) * part, part), part), :].astype(BF16)
        target = send_ref if k % 2 else keep_ref
        target[(k // 2) * part:(k // 2 + 1) * part, :] = rows


def vertex_step(me, weight, cotangent, sums, scale):
    n_row = lax.axis_size("row")
    n, f = cotangent.shape
    half = jax.ShapeDtypeStruct((f // 2, f), BF16)
    smem, vmem = pl.BlockSpec(memory_space=pltpu.SMEM), pl.BlockSpec(memory_space=pltpu.VMEM)
    return pl.pallas_call(
        functools.partial(vertex_kernel, n_row=n_row, n_chunk=len(sums) // 3, scale=scale),
        out_shape=(jax.ShapeDtypeStruct((n, f), BF16), half, half),
        in_specs=[smem] + [vmem] * (2 + len(sums)),
        out_specs=(vmem,) * 3,
        scratch_shapes=[pltpu.VMEM((n, f), BF16), pltpu.VMEM((f, f), F32)],
        compiler_params=pltpu.CompilerParams(vmem_limit_bytes=VMEM_LIMIT),
        cost_estimate=pl.CostEstimate(
            flops=4 * n * f * f, bytes_accessed=4 * 1024 * 1024, transcendentals=n * f),
    )(me, weight, cotangent, *sums)


def join(me, pieces):
    n = len(pieces)
    part, f = pieces[0].shape

    def kernel(me_ref, *refs):
        out_ref = refs[-1]
        for k in range(n):
            at = pl.multiple_of((me_ref[0] ^ k) * part, part)
            out_ref[pl.ds(at, part), :] = refs[k][...].astype(F32)

    smem, vmem = pl.BlockSpec(memory_space=pltpu.SMEM), pl.BlockSpec(memory_space=pltpu.VMEM)
    return pl.pallas_call(
        kernel,
        out_shape=jax.ShapeDtypeStruct((n * part, f), F32),
        in_specs=[smem] + [vmem] * n,
        out_specs=vmem,
        compiler_params=pltpu.CompilerParams(vmem_limit_bytes=VMEM_LIMIT),
    )(me, *pieces)


def reduce_gradient(me, keep, send):
    n_row, n_col = lax.axis_size("row"), lax.axis_size("col")
    part = keep.shape[0] // (n_row // 2)
    chip = keep.astype(F32) + swap(send, "row", 1).astype(F32)
    mine = chip[:part]
    for k in range(1, n_row // 2):
        mine = mine + swap(chip[k * part:(k + 1) * part].astype(BF16), "row", 2 * k).astype(F32)
    bit = 1
    while bit < n_col:
        rounded = mine.astype(BF16)
        if 2 * bit < n_col:
            others = [swap(rounded, "col", m * bit).astype(F32) for m in (1, 2, 3)]
            mine = (rounded.astype(F32) + others[0]) + (others[1] + others[2])
            bit *= 4
        else:
            mine = rounded.astype(F32) + swap(rounded, "col", bit).astype(F32)
            bit *= 2
    rounded = mine.astype(BF16)
    even = [rounded] + [swap(rounded, "row", 2 * k) for k in range(1, n_row // 2)]
    pieces = []
    for p in even:
        pieces += [p, swap(p, "row", 1)]
    return join(me, pieces)


def local(features, tile_values, tile_index, tile_count, weight, cotangent):
    n_row, n_col = lax.axis_size("row"), lax.axis_size("col")
    me = jnp.stack([lax.axis_index("row"), lax.axis_index("col")]).astype(jnp.int32)
    tiles, index, count = tile_values[0, 0], tile_index[0, 0], tile_count[0]
    sums, at = [], 0
    for wide in CHUNKS:
        pieces = gather_row(features[:, at:at + wide])
        at += wide
        keep, send = tile_products(me, index, count, tiles, pieces)
        terms, bit = [], 1
        while bit < n_col:
            got = swap(send, "col", bit)
            bit *= 2
            if bit < n_col:
                half = keep.shape[0] // 2
                send = (keep[half:].astype(F32) + got[half:].astype(F32)).astype(BF16)
                if 2 * bit < n_col:
                    keep = (keep[:half].astype(F32) + got[:half].astype(F32)).astype(BF16)
                else:
                    keep, terms = keep[:half], terms + [got[:half]]
            else:
                terms += [got]
        sums += [keep] + terms
    scale = 1.0 / math.sqrt(cotangent.shape[0] * n_row * n_col)
    output, grad_keep, grad_send = vertex_step(me, weight, cotangent, sums, scale)
    return output, reduce_gradient(me, grad_keep, grad_send)


def solution(mesh):
    placed = (
        P(("col", "row"), None),
        P("row", "col", None, None, None),
        P("row", "col", None),
        P("row", "col"),
        P(),
        P(("row", "col"), None),
    )
    return jax.shard_map(
        local, mesh=mesh, in_specs=placed, out_specs=(P(("row", "col"), None), P()), check_vma=False
    )
```

```python
import functools
import math

import jax
import jax.numpy as jnp
from jax import lax
from jax.experimental import pallas as pl
from jax.experimental.pallas import tpu as pltpu
from jax.sharding import PartitionSpec as P

BLK = 256
RBG = 8
CHUNKS = (256, 256)
COST = 15 * 10**9
VMEM_LIMIT = 48 * 1024 * 1024
F32, BF16 = jnp.float32, jnp.bfloat16


def swap(x, axis, mask):
    return lax.ppermute(x, axis, [(i, i ^ mask) for i in range(lax.axis_size(axis))])


def bit_reversed(i, bits):
    out = 0 * i
    for b in range(bits):
        out = out + (((i >> b) & 1) << (bits - 1 - b))
    return out


def gather_chips(x):
    return [swap(x, "row", k) for k in range(2, lax.axis_size("row"), 2)]


def stage(x):
    def kernel(x_ref, out_ref, sem):
        copy = pltpu.make_async_copy(x_ref, out_ref, sem)
        copy.start()
        copy.wait()

    return pl.pallas_call(
        kernel,
        out_shape=jax.ShapeDtypeStruct(x.shape, x.dtype),
        in_specs=[pl.BlockSpec(memory_space=pl.ANY)],
        out_specs=pl.BlockSpec(memory_space=pltpu.VMEM),
        scratch_shapes=[pltpu.SemaphoreType.DMA],
        compiler_params=pltpu.CompilerParams(vmem_limit_bytes=VMEM_LIMIT),
    )(x)


def tiles_kernel(scalars_ref, tiles_ref, *refs, at, n_row, n_col):
    pieces, out_refs, (picked, total) = refs[:n_row], refs[n_row:-2], refs[-2:]
    rows, wide = pieces[0].shape[0], total.shape[1]
    part = min(BLK, rows)
    own = RBG * BLK // n_col
    step = min(BLK, own)
    bits = n_col.bit_length() - 1
    col_groups = rows * n_row // BLK
    me_row, me_col, count = scalars_ref[0], scalars_ref[1], scalars_ref[2]
    total[...] = jnp.zeros_like(total)
    for k in range(tiles_ref.shape[0]):
        number = scalars_ref[3 + k]
        row_slot, col_slot = number // col_groups, number % col_groups

        @pl.when(k < count)
        def _(k=k, row_slot=row_slot, col_slot=col_slot):
            for j in range(BLK // part):
                first = col_slot * BLK + j * part
                owner = (first // rows) ^ me_row
                block = pl.ds(pl.multiple_of(first % rows, part), part)
                for p in range(n_row):
                    columns = slice(at, at + wide) if p < 2 else slice(None)

                    @pl.when(owner == p)
                    def _(p=p, j=j, block=block, columns=columns):
                        picked[j * part:(j + 1) * part, :] = pieces[p][block, columns]

            product = jnp.dot(tiles_ref[k], picked[...], preferred_element_type=F32)
            for j in range(BLK // step):
                first = row_slot * BLK + j * step
                place = bit_reversed((first // own) ^ me_col, bits) * own + first % own
                place = pl.ds(pl.multiple_of(place, step), step)
                total[place, :] += product[j * step:(j + 1) * step, :]

    quarter = total.shape[0] // 4
    for q, out_ref in enumerate(out_refs):
        out_ref[...] = total[q * quarter:(q + 1) * quarter, :].astype(BF16)


def tile_products(scalars, tiles, pieces, at):
    n_row, n_col = lax.axis_size("row"), lax.axis_size("col")
    wide = pieces[-1].shape[1]
    quarter = jax.ShapeDtypeStruct((RBG * BLK // 4, wide), BF16)
    smem, vmem = pl.BlockSpec(memory_space=pltpu.SMEM), pl.BlockSpec(memory_space=pltpu.VMEM)
    return pl.pallas_call(
        functools.partial(tiles_kernel, at=at, n_row=n_row, n_col=n_col),
        out_shape=(quarter,) * 4,
        in_specs=[smem] + [vmem] * (1 + n_row),
        out_specs=(vmem,) * 4,
        scratch_shapes=[
            pltpu.VMEM((BLK, wide), BF16),
            pltpu.VMEM((RBG * BLK, wide), F32),
        ],
        compiler_params=pltpu.CompilerParams(vmem_limit_bytes=VMEM_LIMIT),
        cost_estimate=pl.CostEstimate(
            flops=2 * tiles.shape[0] * BLK * BLK * wide, bytes_accessed=6 * 1024 * 1024, transcendentals=0),
    )(scalars, tiles, *pieces)


def vertex_kernel(me_ref, weight_ref, cot_ref, *refs, n_row, places, scale):
    *terms, out_ref, keep_ref, send_ref, total, agg, grad = refs
    me_row = me_ref[0]
    total[...] = jnp.zeros_like(total)
    for term, at in zip(terms, places):
        total[:, at:at + term.shape[1]] += term[...].astype(F32)
    agg[...] = total[...].astype(BF16)
    aggregated = agg[...]
    preact = jnp.dot(aggregated, weight_ref[...], preferred_element_type=F32)
    power = jnp.exp(jnp.minimum(preact, 0.0))
    positive = preact > 0
    out_ref[...] = jnp.where(positive, preact, power - 1.0).astype(BF16)
    grad_pre = (cot_ref[...].astype(F32) * jnp.where(positive, 1.0, power)).astype(BF16)
    grad[...] = lax.dot_general(aggregated, grad_pre, (((0,), (0,)), ((), ())), preferred_element_type=F32) * scale
    part = grad.shape[0] // n_row
    for k in range(n_row):
        rows = grad[pl.ds(pl.multiple_of((me_row ^ k) * part, part), part), :].astype(BF16)
        target = send_ref if k % 2 else keep_ref
        target[(k // 2) * part:(k // 2 + 1) * part, :] = rows


def vertex_step(me, weight, cotangent, terms, places, scale):
    n_row = lax.axis_size("row")
    n, f = cotangent.shape
    half = jax.ShapeDtypeStruct((f // 2, f), BF16)
    smem, vmem = pl.BlockSpec(memory_space=pltpu.SMEM), pl.BlockSpec(memory_space=pltpu.VMEM)
    return pl.pallas_call(
        functools.partial(vertex_kernel, n_row=n_row, places=places, scale=scale),
        out_shape=(jax.ShapeDtypeStruct((n, f), BF16), half, half),
        in_specs=[smem] + [vmem] * (2 + len(terms)),
        out_specs=(vmem,) * 3,
        scratch_shapes=[pltpu.VMEM((n, f), F32), pltpu.VMEM((n, f), BF16), pltpu.VMEM((f, f), F32)],
        compiler_params=pltpu.CompilerParams(vmem_limit_bytes=VMEM_LIMIT),
        cost_estimate=pl.CostEstimate(
            flops=4 * n * f * f, bytes_accessed=4 * 1024 * 1024, transcendentals=n * f),
    )(me, weight, cotangent, *terms)


def join(me, pieces):
    n = len(pieces)
    part, f = pieces[0].shape

    def kernel(me_ref, *refs):
        out_ref = refs[-1]
        for k in range(n):
            at = pl.multiple_of((me_ref[0] ^ k) * part, part)
            out_ref[pl.ds(at, part), :] = refs[k][...].astype(F32)

    smem, vmem = pl.BlockSpec(memory_space=pltpu.SMEM), pl.BlockSpec(memory_space=pltpu.VMEM)
    return pl.pallas_call(
        kernel,
        out_shape=jax.ShapeDtypeStruct((n * part, f), F32),
        in_specs=[smem] + [vmem] * n,
        out_specs=vmem,
        compiler_params=pltpu.CompilerParams(vmem_limit_bytes=VMEM_LIMIT),
    )(me, *pieces)


def reduce_gradient(me, keep, send):
    n_row, n_col = lax.axis_size("row"), lax.axis_size("col")
    part = keep.shape[0] // (n_row // 2)
    chip = keep.astype(F32) + swap(send, "row", 1).astype(F32)
    mine = chip[:part]
    for k in range(1, n_row // 2):
        mine = mine + swap(chip[k * part:(k + 1) * part].astype(BF16), "row", 2 * k).astype(F32)
    bit = 1
    while bit < n_col:
        rounded = mine.astype(BF16)
        if 2 * bit < n_col:
            others = [swap(rounded, "col", m * bit).astype(F32) for m in (1, 2, 3)]
            mine = (rounded.astype(F32) + others[0]) + (others[1] + others[2])
            bit *= 4
        else:
            mine = rounded.astype(F32) + swap(rounded, "col", bit).astype(F32)
            bit *= 2
    rounded = mine.astype(BF16)
    even = [rounded] + [swap(rounded, "row", 2 * k) for k in range(1, n_row // 2)]
    pieces = []
    for p in even:
        pieces += [p, swap(p, "row", 1)]
    return join(me, pieces)


def plus(*terms):
    return sum((t.astype(F32) for t in terms[1:]), terms[0].astype(F32)).astype(BF16)


def sum_terms(*terms):
    def kernel(*refs):
        total = refs[0][...].astype(F32)
        for ref in refs[1:-1]:
            total += ref[...].astype(F32)
        refs[-1][...] = total.astype(BF16)

    vmem = pl.BlockSpec(memory_space=pltpu.VMEM)
    return pl.pallas_call(
        kernel,
        out_shape=jax.ShapeDtypeStruct(terms[0].shape, BF16),
        in_specs=[vmem] * len(terms),
        out_specs=vmem,
        compiler_params=pltpu.CompilerParams(vmem_limit_bytes=VMEM_LIMIT),
        cost_estimate=pl.CostEstimate(flops=COST, bytes_accessed=4 * terms[0].size * 2, transcendentals=0),
    )(*terms)


def local(features, tile_values, tile_index, tile_count, weight, cotangent):
    n_row, n_col = lax.axis_size("row"), lax.axis_size("col")
    me = jnp.stack([lax.axis_index("row"), lax.axis_index("col")]).astype(jnp.int32)
    tiles = stage(tile_values[0, 0])
    scalars = jnp.concatenate([me, tile_count[0], tile_index[0, 0]])
    starts = [sum(CHUNKS[:j]) for j in range(len(CHUNKS))]
    parts = [features[:, at:at + wide] for at, wide in zip(starts, CHUNKS)]
    own, tiles, scalars = lax.optimization_barrier((features, tiles, scalars))
    core = swap(own, "row", 1)
    keep, terms = (), []
    for part, at in zip(parts, starts):
        part, *keep = lax.optimization_barrier((part, *keep))
        pieces = [features, core]
        for block in gather_chips(part):
            pieces += [block, swap(block, "row", 1)]
        *keep, near, away = tile_products(scalars, tiles, pieces, at)
        if terms:
            stay, far, got_near = terms
            before = sum_terms(stay, got_near)
            away, before = lax.optimization_barrier((away, before))
        got = swap(away, "col", 1)
        send = plus(keep[1], got)
        if terms:
            before = sum_terms(before, far)
            send, before = lax.optimization_barrier((send, before))
            near, got = lax.optimization_barrier((near, got))
        terms = [keep[0], swap(send, "col", 2), swap(near, "col", 1)]
    terms = [(before, 0)] + [(t, at) for t in terms]
    if n_col > 4:
        bit = 4
        mine = jnp.concatenate([plus(*(t for t, place in terms if place == at)) for at in starts], axis=1)
        while bit < n_col:
            half = mine.shape[0] // 2
            mine = plus(mine[:half], swap(mine[half:], "col", bit))
            bit *= 2
        terms = [(mine, 0)]
    terms, places = zip(*terms)
    scale = 1.0 / math.sqrt(cotangent.shape[0] * n_row * n_col)
    output, grad_keep, grad_send = vertex_step(me, weight, cotangent, terms, places, scale)
    return output, reduce_gradient(me, grad_keep, grad_send)


def solution(mesh):
    placed = (
        P(("col", "row"), None),
        P("row", "col", None, None, None),
        P("row", "col", None),
        P("row", "col"),
        P(),
        P(("row", "col"), None),
    )
    return jax.shard_map(
        local, mesh=mesh, in_specs=placed, out_specs=(P(("row", "col"), None), P()), check_vma=False
    )
```

```python
import functools
import math

import jax
import jax.numpy as jnp
from jax import lax
from jax.experimental import pallas as pl
from jax.experimental.pallas import tpu as pltpu
from jax.sharding import PartitionSpec as P

BLK = 256
RBG = 8
CHUNKS = (256, 256)
FIELD = 256
COST = 15 * 10**9
VMEM_LIMIT = 48 * 1024 * 1024
F32, BF16 = jnp.float32, jnp.bfloat16


def swap(x, axis, mask):
    return lax.ppermute(x, axis, [(i, i ^ mask) for i in range(lax.axis_size(axis))])


def bit_reversed(i, bits):
    out = 0 * i
    for b in range(bits):
        out = out + (((i >> b) & 1) << (bits - 1 - b))
    return out


def gather_chips(early, late):
    return [swap(early if k & (k - 1) == 0 else late, "row", k) for k in range(2, lax.axis_size("row"), 2)]


def relay_chips(x, *later):
    half = x.shape[0] // 2
    masks = sorted(range(2, lax.axis_size("row"), 2), key=lambda k: (bin(k).count("1"), k))
    near = [k for k in masks if k & (k - 1) == 0]
    halves = {}
    for early in (True, False):
        for k in near:
            h = int((k != near[0]) == early)
            halves[k, h] = swap(x[h * half:(h + 1) * half], "row", k)
    first = [(k, int(k != near[0])) for k in near]
    arrived, later = lax.optimization_barrier(([halves[key] for key in first], later))
    halves.update(zip(first, arrived))
    for k in masks[len(near):]:
        low, high = k & -k, 1 << (k.bit_length() - 1)
        halves[k, 0] = swap(halves[k ^ high, 0], "row", high)
        halves[k, 1] = swap(halves[k ^ low, 1], "row", low)
    return [jnp.concatenate([halves[k, 0], halves[k, 1]]) for k in sorted(masks)], *later


def stage(x):
    def kernel(x_ref, out_ref, sem):
        copy = pltpu.make_async_copy(x_ref, out_ref, sem)
        copy.start()
        copy.wait()

    return pl.pallas_call(
        kernel,
        out_shape=jax.ShapeDtypeStruct(x.shape, x.dtype),
        in_specs=[pl.BlockSpec(memory_space=pl.ANY)],
        out_specs=pl.BlockSpec(memory_space=pltpu.VMEM),
        scratch_shapes=[pltpu.SemaphoreType.DMA],
        compiler_params=pltpu.CompilerParams(vmem_limit_bytes=VMEM_LIMIT),
    )(x)


def slot_numbers(index, count, rows):
    n_row, n_col = lax.axis_size("row"), lax.axis_size("col")
    own = RBG * BLK // n_col
    part, bits = min(BLK, rows, own), n_col.bit_length() - 1
    col_groups = rows * n_row // BLK
    live = jnp.arange(index.shape[0]) < count
    along = jnp.arange(0, BLK, part)
    first = (index % col_groups * BLK)[:, None] + along
    source = jnp.where(live[:, None], (first // rows) ^ lax.axis_index("row"), n_row)
    target = (index // col_groups * BLK)[:, None] + along
    place = bit_reversed((target // own) ^ lax.axis_index("col"), bits) * own + target % own
    numbers = (source + FIELD * (first % rows // part) + FIELD * FIELD * (place // part)).reshape(-1)
    return jnp.broadcast_to(jnp.pad(numbers.astype(jnp.int32), (0, 128 - numbers.size)), (8, 128))


def tiles_kernel(numbers_ref, tiles_ref, *refs, at, n_row, part):
    pieces, out_refs, (picked, total) = refs[:n_row], refs[n_row:-2], refs[-2:]
    kmax = tiles_ref.shape[0]
    wide = total.shape[1]
    parts = BLK // part
    total[...] = jnp.zeros_like(total)
    places = []
    for i in range(kmax * parts):
        k, to = i // parts, pl.ds(i % parts * part, part)
        number = numbers_ref[0, i]
        source, row = number & (FIELD - 1), (number // FIELD) & (FIELD - 1)
        places.append(pl.ds(pl.multiple_of(number // (FIELD * FIELD) * part, part), part))
        block = pl.ds(pl.multiple_of(row * part, part), part)

        @pl.when(source == n_row)
        def _(k=k, to=to):
            picked[k, to, :] = jnp.zeros((part, wide), BF16)

        for p in range(n_row):
            columns = slice(at, at + wide) if p < 2 else slice(None)

            @pl.when(source == p)
            def _(k=k, to=to, p=p, block=block, columns=columns):
                picked[k, to, :] = pieces[p][block, columns]

    for k in range(kmax):
        product = jnp.dot(tiles_ref[k], picked[k], preferred_element_type=F32)
        for j in range(parts):
            total[places[k * parts + j], :] += product[j * part:(j + 1) * part, :]

    quarter = total.shape[0] // 4
    for q, out_ref in enumerate(out_refs):
        out_ref[...] = total[q * quarter:(q + 1) * quarter, :].astype(BF16)


def tile_products(numbers, tiles, pieces, at):
    n_row, n_col = lax.axis_size("row"), lax.axis_size("col")
    wide = pieces[-1].shape[1]
    quarter = jax.ShapeDtypeStruct((RBG * BLK // 4, wide), BF16)
    vmem = pl.BlockSpec(memory_space=pltpu.VMEM)
    return pl.pallas_call(
        functools.partial(tiles_kernel, at=at, n_row=n_row, part=min(BLK, pieces[0].shape[0], RBG * BLK // n_col)),
        out_shape=(quarter,) * 4,
        in_specs=[vmem] * (2 + n_row),
        out_specs=(vmem,) * 4,
        scratch_shapes=[
            pltpu.VMEM((tiles.shape[0], BLK, wide), BF16),
            pltpu.VMEM((RBG * BLK, wide), F32),
        ],
        compiler_params=pltpu.CompilerParams(vmem_limit_bytes=VMEM_LIMIT),
        cost_estimate=pl.CostEstimate(
            flops=2 * tiles.shape[0] * BLK * BLK * wide, bytes_accessed=6 * 1024 * 1024, transcendentals=0),
    )(numbers, tiles, *pieces)


def early_part(terms, weight, at, before):
    n, wide = terms[0].shape
    f = weight.shape[1]

    def kernel(weight_ref, *refs):
        *terms, agg_ref, pre_ref = refs
        if before is not None:
            before_ref, *terms = terms
        total = terms[0][...].astype(F32)
        for term in terms[1:]:
            total += term[...].astype(F32)
        agg_ref[...] = total.astype(BF16)
        share = jnp.dot(agg_ref[...], weight_ref[at:at + wide, :], preferred_element_type=F32)
        pre_ref[...] = share if before is None else before_ref[...] + share

    vmem = pl.BlockSpec(memory_space=pltpu.VMEM)
    inputs = (weight, *([] if before is None else [before]), *terms)
    return pl.pallas_call(
        kernel,
        out_shape=(jax.ShapeDtypeStruct((n, wide), BF16), jax.ShapeDtypeStruct((n, f), F32)),
        in_specs=[vmem] * len(inputs),
        out_specs=(vmem,) * 2,
        compiler_params=pltpu.CompilerParams(vmem_limit_bytes=VMEM_LIMIT),
        cost_estimate=pl.CostEstimate(flops=COST, bytes_accessed=4 * n * f, transcendentals=0),
    )(*inputs)


def vertex_kernel(weight_ref, cot_ref, pre_ref, *refs, n_row, n_early, scale):
    early, (*terms, out_ref, keep_ref, send_ref, output, grad, sem) = refs[:n_early], refs[n_early:]
    me_row = lax.axis_index("row")
    cut = grad.shape[0] - terms[0].shape[1]
    total = terms[0][...].astype(F32)
    for term in terms[1:]:
        total += term[...].astype(F32)
    last = total.astype(BF16)
    preact = pre_ref[...] + jnp.dot(last, weight_ref[cut:, :], preferred_element_type=F32)
    power = jnp.exp(jnp.minimum(preact, 0.0))
    positive = preact > 0
    output[...] = jnp.where(positive, preact, power - 1.0).astype(BF16)
    copy = pltpu.make_async_copy(output, out_ref, sem)
    copy.start()
    grad_pre = (cot_ref[...].astype(F32) * jnp.where(positive, 1.0, power)).astype(BF16)
    over_rows = (((0,), (0,)), ((), ()))
    at = 0
    for aggregated in [ref[...] for ref in early] + [last]:
        wide = aggregated.shape[1]
        grad[at:at + wide, :] = lax.dot_general(
            aggregated, grad_pre, over_rows, preferred_element_type=F32) * scale
        at += wide
    part = grad.shape[0] // n_row
    for k in range(n_row):
        rows = grad[pl.ds(pl.multiple_of((me_row ^ k) * part, part), part), :].astype(BF16)
        target = send_ref if k % 2 else keep_ref
        target[(k // 2) * part:(k // 2 + 1) * part, :] = rows
    copy.wait()


def vertex_step(weight, cotangent, pre, early, terms, scale):
    n_row = lax.axis_size("row")
    n, f = cotangent.shape
    half = jax.ShapeDtypeStruct((f // 2, f), BF16)
    vmem = pl.BlockSpec(memory_space=pltpu.VMEM)
    return pl.pallas_call(
        functools.partial(vertex_kernel, n_row=n_row, n_early=len(early), scale=scale),
        out_shape=(jax.ShapeDtypeStruct((n, f), BF16), half, half),
        in_specs=[vmem] * (3 + len(early) + len(terms)),
        out_specs=(pl.BlockSpec(memory_space=pl.ANY), vmem, vmem),
        scratch_shapes=[pltpu.VMEM((n, f), BF16), pltpu.VMEM((f, f), F32), pltpu.SemaphoreType.DMA],
        compiler_params=pltpu.CompilerParams(vmem_limit_bytes=VMEM_LIMIT),
        cost_estimate=pl.CostEstimate(
            flops=4 * n * f * f, bytes_accessed=4 * 1024 * 1024, transcendentals=n * f),
    )(weight, cotangent, pre, *early, *terms)


def join(pieces):
    n = len(pieces)
    part, f = pieces[0].shape

    def kernel(*refs):
        out_ref = refs[-1]
        me_row = lax.axis_index("row")
        for k in range(n):
            at = pl.multiple_of((me_row ^ k) * part, part)
            out_ref[pl.ds(at, part), :] = refs[k][...].astype(F32)

    vmem = pl.BlockSpec(memory_space=pltpu.VMEM)
    return pl.pallas_call(
        kernel,
        out_shape=jax.ShapeDtypeStruct((n * part, f), F32),
        in_specs=[vmem] * n,
        out_specs=vmem,
        compiler_params=pltpu.CompilerParams(vmem_limit_bytes=VMEM_LIMIT),
    )(*pieces)


def reduce_gradient(keep, send):
    n_row, n_col = lax.axis_size("row"), lax.axis_size("col")
    part = keep.shape[0] // (n_row // 2)
    chip = keep.astype(F32) + swap(send, "row", 1).astype(F32)
    mine = chip[:part]
    for k in range(1, n_row // 2):
        mine = mine + swap(chip[k * part:(k + 1) * part].astype(BF16), "row", 2 * k).astype(F32)
    rounded, bit = mine.astype(BF16), 1
    while bit < n_col:
        if 2 * bit < n_col:
            others = [swap(rounded, "col", m * bit) for m in (1, 2, 3)]
            rounded = ((rounded.astype(F32) + others[0].astype(F32)) + (others[1].astype(F32) + others[2].astype(F32))).astype(BF16)
            bit *= 4
        else:
            rounded = plus(rounded, swap(rounded, "col", bit))
            bit *= 2
    pieces = []
    for k in range(0, n_row, 2):
        piece = swap(rounded, "row", k) if k else rounded
        pieces += [piece, swap(piece, "row", 1)]
    return join(pieces)


def plus(*terms):
    return sum((t.astype(F32) for t in terms[1:]), terms[0].astype(F32)).astype(BF16)


def finish(terms):
    n_col, bit = lax.axis_size("col"), 4
    while bit < n_col:
        mine = plus(*terms)
        half = mine.shape[0] // 2
        terms = mine[:half], swap(mine[half:], "col", bit)
        bit *= 2
    return terms


def hold(x):
    def kernel(x_ref, out_ref):
        out_ref[...] = x_ref[...]

    vmem = pl.BlockSpec(memory_space=pltpu.VMEM)
    return pl.pallas_call(
        kernel,
        out_shape=jax.ShapeDtypeStruct(x.shape, x.dtype),
        in_specs=[vmem],
        out_specs=vmem,
        compiler_params=pltpu.CompilerParams(vmem_limit_bytes=VMEM_LIMIT),
        cost_estimate=pl.CostEstimate(flops=COST, bytes_accessed=4 * x.size, transcendentals=0),
    )(x)


def local(features, tile_values, tile_index, tile_count, weight, cotangent):
    n_row, n_col = lax.axis_size("row"), lax.axis_size("col")
    starts = [sum(CHUNKS[:j]) for j in range(len(CHUNKS))]
    blocks, own, tiles, index, count = relay_chips(
        features[:, :CHUNKS[0]], features, tile_values[0, 0], tile_index[0, 0], tile_count[0, 0])
    numbers = slot_numbers(index, count, features.shape[0])
    tiles = stage(tiles)
    core = swap(own, "row", 1)
    keep, summed, pre = (), [], None
    for at, wide in zip(starts, CHUNKS):
        final = at + wide == features.shape[1]
        if at:
            early, *blocks = lax.optimization_barrier((features, *blocks))
            late, *keep = lax.optimization_barrier((features, *keep))
            blocks = gather_chips(early[:, at:at + wide], late[:, at:at + wide])
        pieces = [own, core]
        for block in blocks:
            pieces += [block, swap(block, "row", 1)]
        *keep, near, away = tile_products(numbers, tiles, pieces, at)
        if at:
            away, terms[0] = lax.optimization_barrier((away, hold(terms[0])))
        got = swap(away, "col", 1)
        send = plus(keep[1], got)
        if at:
            aggregated, pre = early_part(finish(terms), weight, done, pre)
            send, aggregated, pre = lax.optimization_barrier((send, aggregated, pre))
            summed.append(aggregated)
        if final:
            near, got = lax.optimization_barrier((near, got))
        cut = near.shape[0] // (2 if final else 1)
        arrived = [swap(near[i:i + cut], "col", 1) for i in range(0, near.shape[0], cut)]
        terms, done = [keep[0], swap(send, "col", 2), jnp.concatenate(arrived)], at
    scale = 1.0 / math.sqrt(cotangent.shape[0] * n_row * n_col)
    output, grad_keep, grad_send = vertex_step(weight, cotangent, pre, summed, finish(terms), scale)
    return output, reduce_gradient(grad_keep, grad_send)


def solution(mesh):
    placed = (
        P(("col", "row"), None),
        P("row", "col", None, None, None),
        P("row", "col", None),
        P("row", "col"),
        P(),
        P(("row", "col"), None),
    )
    return jax.shard_map(
        local, mesh=mesh, in_specs=placed, out_specs=(P(("row", "col"), None), P()), check_vma=False
    )
```

```python
import functools
import math

import jax
import jax.numpy as jnp
from jax import lax
from jax.experimental import pallas as pl
from jax.experimental.pallas import tpu as pltpu
from jax.sharding import PartitionSpec as P

BLK = 256
RBG = 8
CHUNKS = (256, 256)
FIELD = 256
COST = 15 * 10**9
VMEM_LIMIT = 48 * 1024 * 1024
F32, BF16 = jnp.float32, jnp.bfloat16


def swap(x, axis, mask):
    return lax.ppermute(x, axis, [(i, i ^ mask) for i in range(lax.axis_size(axis))])


def bit_reversed(i, bits):
    out = 0 * i
    for b in range(bits):
        out = out + (((i >> b) & 1) << (bits - 1 - b))
    return out


def gather_chips(early, late):
    return [swap(early if k & (k - 1) == 0 else late, "row", k) for k in range(2, lax.axis_size("row"), 2)]


def relay_chips(x, *later):
    half = x.shape[0] // 2
    masks = sorted(range(2, lax.axis_size("row"), 2), key=lambda k: (bin(k).count("1"), k))
    near = [k for k in masks if k & (k - 1) == 0]
    halves = {}
    for early in (True, False):
        for k in near:
            h = int((k != near[0]) == early)
            halves[k, h] = swap(x[h * half:(h + 1) * half], "row", k)
    first = [(k, int(k != near[0])) for k in near]
    arrived, later = lax.optimization_barrier(([halves[key] for key in first], later))
    halves.update(zip(first, arrived))
    for k in masks[len(near):]:
        low, high = k & -k, 1 << (k.bit_length() - 1)
        halves[k, 0] = swap(halves[k ^ high, 0], "row", high)
        halves[k, 1] = swap(halves[k ^ low, 1], "row", low)
    return [jnp.concatenate([halves[k, 0], halves[k, 1]]) for k in sorted(masks)], *later


def stage(x):
    def kernel(x_ref, out_ref, sem):
        copy = pltpu.make_async_copy(x_ref, out_ref, sem)
        copy.start()
        copy.wait()

    return pl.pallas_call(
        kernel,
        out_shape=jax.ShapeDtypeStruct(x.shape, x.dtype),
        in_specs=[pl.BlockSpec(memory_space=pl.ANY)],
        out_specs=pl.BlockSpec(memory_space=pltpu.VMEM),
        scratch_shapes=[pltpu.SemaphoreType.DMA],
        compiler_params=pltpu.CompilerParams(vmem_limit_bytes=VMEM_LIMIT),
    )(x)


def slot_numbers(index, count, rows):
    n_row, n_col = lax.axis_size("row"), lax.axis_size("col")
    own = RBG * BLK // n_col
    part, bits = min(BLK, rows, own), n_col.bit_length() - 1
    col_groups = rows * n_row // BLK
    live = jnp.arange(index.shape[0]) < count
    along = jnp.arange(0, BLK, part)
    first = (index % col_groups * BLK)[:, None] + along
    source = jnp.where(live[:, None], (first // rows) ^ lax.axis_index("row"), n_row)
    target = (index // col_groups * BLK)[:, None] + along
    place = bit_reversed((target // own) ^ lax.axis_index("col"), bits) * own + target % own
    numbers = (source + FIELD * (first % rows // part) + FIELD * FIELD * (place // part)).reshape(-1)
    return jnp.broadcast_to(jnp.pad(numbers.astype(jnp.int32), (0, 128 - numbers.size)), (8, 128))


def tiles_kernel(numbers_ref, tiles_ref, *refs, at, n_row, part):
    pieces, out_refs, (picked, total) = refs[:n_row], refs[n_row:-2], refs[-2:]
    kmax = tiles_ref.shape[0]
    wide = total.shape[1]
    parts = BLK // part
    total[...] = jnp.zeros_like(total)
    places = []
    for i in range(kmax * parts):
        k, to = i // parts, pl.ds(i % parts * part, part)
        number = numbers_ref[0, i]
        source, row = number & (FIELD - 1), (number // FIELD) & (FIELD - 1)
        places.append(pl.ds(pl.multiple_of(number // (FIELD * FIELD) * part, part), part))
        block = pl.ds(pl.multiple_of(row * part, part), part)

        @pl.when(source == n_row)
        def _(k=k, to=to):
            picked[k, to, :] = jnp.zeros((part, wide), BF16)

        for p in range(n_row):
            columns = slice(at, at + wide) if p < 2 else slice(None)

            @pl.when(source == p)
            def _(k=k, to=to, p=p, block=block, columns=columns):
                picked[k, to, :] = pieces[p][block, columns]

    for k in range(kmax):
        product = jnp.dot(tiles_ref[k], picked[k], preferred_element_type=F32)
        for j in range(parts):
            total[places[k * parts + j], :] += product[j * part:(j + 1) * part, :]

    quarter = total.shape[0] // 4
    for q, out_ref in enumerate(out_refs):
        out_ref[...] = total[q * quarter:(q + 1) * quarter, :].astype(BF16)


def tile_products(numbers, tiles, pieces, at):
    n_row, n_col = lax.axis_size("row"), lax.axis_size("col")
    wide = pieces[-1].shape[1]
    quarter = jax.ShapeDtypeStruct((RBG * BLK // 4, wide), BF16)
    vmem = pl.BlockSpec(memory_space=pltpu.VMEM)
    return pl.pallas_call(
        functools.partial(tiles_kernel, at=at, n_row=n_row, part=min(BLK, pieces[0].shape[0], RBG * BLK // n_col)),
        out_shape=(quarter,) * 4,
        in_specs=[vmem] * (2 + n_row),
        out_specs=(vmem,) * 4,
        scratch_shapes=[
            pltpu.VMEM((tiles.shape[0], BLK, wide), BF16),
            pltpu.VMEM((RBG * BLK, wide), F32),
        ],
        compiler_params=pltpu.CompilerParams(vmem_limit_bytes=VMEM_LIMIT),
        cost_estimate=pl.CostEstimate(
            flops=2 * tiles.shape[0] * BLK * BLK * wide, bytes_accessed=6 * 1024 * 1024, transcendentals=0),
    )(numbers, tiles, *pieces)


def early_part(terms, weight, at, before):
    n, wide = terms[0].shape
    f = weight.shape[1]

    def kernel(weight_ref, *refs):
        *terms, agg_ref, pre_ref = refs
        if before is not None:
            before_ref, *terms = terms
        total = terms[0][...].astype(F32)
        for term in terms[1:]:
            total += term[...].astype(F32)
        agg_ref[...] = total.astype(BF16)
        share = jnp.dot(agg_ref[...], weight_ref[at:at + wide, :], preferred_element_type=F32)
        pre_ref[...] = share if before is None else before_ref[...] + share

    vmem = pl.BlockSpec(memory_space=pltpu.VMEM)
    inputs = (weight, *([] if before is None else [before]), *terms)
    return pl.pallas_call(
        kernel,
        out_shape=(jax.ShapeDtypeStruct((n, wide), BF16), jax.ShapeDtypeStruct((n, f), F32)),
        in_specs=[vmem] * len(inputs),
        out_specs=(vmem,) * 2,
        compiler_params=pltpu.CompilerParams(vmem_limit_bytes=VMEM_LIMIT),
        cost_estimate=pl.CostEstimate(flops=COST, bytes_accessed=4 * n * f, transcendentals=0),
    )(*inputs)


def vertex_kernel(weight_ref, cot_ref, pre_ref, *refs, n_row, n_early, scale):
    early, (*terms, out_ref, keep_ref, send_ref, output, grad, sem) = refs[:n_early], refs[n_early:]
    me_row = lax.axis_index("row")
    cut = grad.shape[0] - terms[0].shape[1]
    total = terms[0][...].astype(F32)
    for term in terms[1:]:
        total += term[...].astype(F32)
    last = total.astype(BF16)
    preact = pre_ref[...] + jnp.dot(last, weight_ref[cut:, :], preferred_element_type=F32)
    power = jnp.exp(jnp.minimum(preact, 0.0))
    positive = preact > 0
    output[...] = jnp.where(positive, preact, power - 1.0).astype(BF16)
    copy = pltpu.make_async_copy(output, out_ref, sem)
    copy.start()
    grad_pre = (cot_ref[...].astype(F32) * jnp.where(positive, 1.0, power)).astype(BF16)
    over_rows = (((0,), (0,)), ((), ()))
    at = 0
    for aggregated in [ref[...] for ref in early] + [last]:
        wide = aggregated.shape[1]
        grad[at:at + wide, :] = lax.dot_general(
            aggregated, grad_pre, over_rows, preferred_element_type=F32) * scale
        at += wide
    part = grad.shape[0] // n_row
    for k in range(n_row):
        rows = grad[pl.ds(pl.multiple_of((me_row ^ k) * part, part), part), :].astype(BF16)
        target = send_ref if k % 2 else keep_ref
        target[(k // 2) * part:(k // 2 + 1) * part, :] = rows
    copy.wait()


def vertex_step(weight, cotangent, pre, early, terms, scale):
    n_row = lax.axis_size("row")
    n, f = cotangent.shape
    half = jax.ShapeDtypeStruct((f // 2, f), BF16)
    vmem = pl.BlockSpec(memory_space=pltpu.VMEM)
    return pl.pallas_call(
        functools.partial(vertex_kernel, n_row=n_row, n_early=len(early), scale=scale),
        out_shape=(jax.ShapeDtypeStruct((n, f), BF16), half, half),
        in_specs=[vmem] * (3 + len(early) + len(terms)),
        out_specs=(pl.BlockSpec(memory_space=pl.ANY), vmem, vmem),
        scratch_shapes=[pltpu.VMEM((n, f), BF16), pltpu.VMEM((f, f), F32), pltpu.SemaphoreType.DMA],
        compiler_params=pltpu.CompilerParams(vmem_limit_bytes=VMEM_LIMIT),
        cost_estimate=pl.CostEstimate(
            flops=4 * n * f * f, bytes_accessed=4 * 1024 * 1024, transcendentals=n * f),
    )(weight, cotangent, pre, *early, *terms)


def join(pieces):
    n = len(pieces)
    part, f = pieces[0].shape

    def kernel(*refs):
        out_ref = refs[-1]
        me_row = lax.axis_index("row")
        for k in range(n):
            at = pl.multiple_of((me_row ^ k) * part, part)
            out_ref[pl.ds(at, part), :] = refs[k][...].astype(F32)

    vmem = pl.BlockSpec(memory_space=pltpu.VMEM)
    return pl.pallas_call(
        kernel,
        out_shape=jax.ShapeDtypeStruct((n * part, f), F32),
        in_specs=[vmem] * n,
        out_specs=vmem,
        compiler_params=pltpu.CompilerParams(vmem_limit_bytes=VMEM_LIMIT),
    )(*pieces)


def reduce_gradient(keep, send):
    n_row, n_col = lax.axis_size("row"), lax.axis_size("col")
    part = keep.shape[0] // (n_row // 2)
    chip = keep.astype(F32) + swap(send, "row", 1).astype(F32)
    mine = chip[:part]
    for k in range(1, n_row // 2):
        mine = mine + swap(chip[k * part:(k + 1) * part].astype(BF16), "row", 2 * k).astype(F32)
    rounded, bit = mine.astype(BF16), 1
    while bit < n_col:
        if 2 * bit < n_col:
            others = [swap(rounded, "col", m * bit) for m in (1, 2, 3)]
            rounded = ((rounded.astype(F32) + others[0].astype(F32)) + (others[1].astype(F32) + others[2].astype(F32))).astype(BF16)
            bit *= 4
        else:
            rounded = plus(rounded, swap(rounded, "col", bit))
            bit *= 2
    pieces = []
    for k in range(0, n_row, 2):
        piece = swap(rounded, "row", k) if k else rounded
        pieces += [piece, swap(piece, "row", 1)]
    return join(pieces)


def plus(*terms):
    return sum((t.astype(F32) for t in terms[1:]), terms[0].astype(F32)).astype(BF16)


def finish(terms):
    n_col, bit = lax.axis_size("col"), 4
    while bit < n_col:
        mine = plus(*terms)
        half = mine.shape[0] // 2
        terms = mine[:half], swap(mine[half:], "col", bit)
        bit *= 2
    return terms


def hold(x):
    def kernel(x_ref, out_ref):
        out_ref[...] = x_ref[...]

    vmem = pl.BlockSpec(memory_space=pltpu.VMEM)
    return pl.pallas_call(
        kernel,
        out_shape=jax.ShapeDtypeStruct(x.shape, x.dtype),
        in_specs=[vmem],
        out_specs=vmem,
        compiler_params=pltpu.CompilerParams(vmem_limit_bytes=VMEM_LIMIT),
        cost_estimate=pl.CostEstimate(flops=COST, bytes_accessed=4 * x.size, transcendentals=0),
    )(x)


def local(features, tile_values, tile_index, tile_count, weight, cotangent):
    n_row, n_col = lax.axis_size("row"), lax.axis_size("col")
    starts = [sum(CHUNKS[:j]) for j in range(len(CHUNKS))]
    blocks, own, tiles, index, count = relay_chips(
        features[:, :CHUNKS[0]], features, tile_values[0, 0], tile_index[0, 0], tile_count[0, 0])
    numbers = slot_numbers(index, count, features.shape[0])
    tiles = stage(tiles)
    core = swap(own, "row", 1)
    keep, summed, pre = (), [], None
    for at, wide in zip(starts, CHUNKS):
        final = at + wide == features.shape[1]
        if at:
            early, *blocks = lax.optimization_barrier((features, *blocks))
            late, *keep = lax.optimization_barrier((features, *keep))
            blocks = gather_chips(early[:, at:at + wide], late[:, at:at + wide])
        pieces = [own, core]
        for block in blocks:
            pieces += [block, swap(block, "row", 1)]
        *keep, near, away = tile_products(numbers, tiles, pieces, at)
        if at:
            away, terms[0] = lax.optimization_barrier((away, hold(terms[0])))
        got = swap(away, "col", 1)
        send = plus(keep[1], got)
        if at:
            aggregated, pre = early_part(finish(terms), weight, done, pre)
            send, aggregated, pre = lax.optimization_barrier((send, aggregated, pre))
            summed.append(aggregated)
        near, got = lax.optimization_barrier((near, got))
        cut = near.shape[0] // (2 if final else 1)
        arrived = [swap(near[i:i + cut], "col", 1) for i in range(0, near.shape[0], cut)]
        terms, done = [keep[0], swap(send, "col", 2), jnp.concatenate(arrived)], at
    scale = 1.0 / math.sqrt(cotangent.shape[0] * n_row * n_col)
    output, grad_keep, grad_send = vertex_step(weight, cotangent, pre, summed, finish(terms), scale)
    return output, reduce_gradient(grad_keep, grad_send)


def solution(mesh):
    placed = (
        P(("col", "row"), None),
        P("row", "col", None, None, None),
        P("row", "col", None),
        P("row", "col"),
        P(),
        P(("row", "col"), None),
    )
    return jax.shard_map(
        local, mesh=mesh, in_specs=placed, out_specs=(P(("row", "col"), None), P()), check_vma=False
    )
```

```python
import functools
import math

import jax
import jax.numpy as jnp
from jax import lax
from jax.experimental import pallas as pl
from jax.experimental.pallas import tpu as pltpu
from jax.sharding import PartitionSpec as P

BLK = 256
RBG = 8
CHUNKS = (256, 256)
FIELD = 256
COST = 15 * 10**9
VMEM_LIMIT = 48 * 1024 * 1024
F32, BF16 = jnp.float32, jnp.bfloat16


def swap(x, axis, mask):
    return lax.ppermute(x, axis, [(i, i ^ mask) for i in range(lax.axis_size(axis))])


def bit_reversed(i, bits):
    out = 0 * i
    for b in range(bits):
        out = out + (((i >> b) & 1) << (bits - 1 - b))
    return out


def gather_chips(early, late):
    return [swap(early if k & (k - 1) == 0 else late, "row", k) for k in range(2, lax.axis_size("row"), 2)]


def relay_chips(x, *later):
    half = x.shape[0] // 2
    masks = sorted(range(2, lax.axis_size("row"), 2), key=lambda k: (bin(k).count("1"), k))
    near = [k for k in masks if k & (k - 1) == 0]
    halves = {}
    for early in (True, False):
        for k in near:
            h = int((k != near[0]) == early)
            halves[k, h] = swap(x[h * half:(h + 1) * half], "row", k)
    first = [(k, int(k != near[0])) for k in near]
    arrived, later = lax.optimization_barrier(([halves[key] for key in first], later))
    halves.update(zip(first, arrived))
    for k in masks[len(near):]:
        low, high = k & -k, 1 << (k.bit_length() - 1)
        halves[k, 0] = swap(halves[k ^ high, 0], "row", high)
        halves[k, 1] = swap(halves[k ^ low, 1], "row", low)
    return [jnp.concatenate([halves[k, 0], halves[k, 1]]) for k in sorted(masks)], *later


def stage(x):
    def kernel(x_ref, out_ref, sem):
        copy = pltpu.make_async_copy(x_ref, out_ref, sem)
        copy.start()
        copy.wait()

    return pl.pallas_call(
        kernel,
        out_shape=jax.ShapeDtypeStruct(x.shape, x.dtype),
        in_specs=[pl.BlockSpec(memory_space=pl.ANY)],
        out_specs=pl.BlockSpec(memory_space=pltpu.VMEM),
        scratch_shapes=[pltpu.SemaphoreType.DMA],
        compiler_params=pltpu.CompilerParams(vmem_limit_bytes=VMEM_LIMIT),
    )(x)


def slot_numbers(index, count, rows):
    n_row, n_col = lax.axis_size("row"), lax.axis_size("col")
    own = RBG * BLK // n_col
    part, bits = min(BLK, rows, own), n_col.bit_length() - 1
    col_groups = rows * n_row // BLK
    live = jnp.arange(index.shape[0]) < count
    along = jnp.arange(0, BLK, part)
    first = (index % col_groups * BLK)[:, None] + along
    source = jnp.where(live[:, None], (first // rows) ^ lax.axis_index("row"), n_row)
    target = (index // col_groups * BLK)[:, None] + along
    place = bit_reversed((target // own) ^ lax.axis_index("col"), bits) * own + target % own
    numbers = (source + FIELD * (first % rows // part) + FIELD * FIELD * (place // part)).reshape(-1)
    return jnp.broadcast_to(jnp.pad(numbers.astype(jnp.int32), (0, 128 - numbers.size)), (8, 128))


def tiles_kernel(numbers_ref, tiles_ref, *refs, at, n_row, part):
    pieces, out_refs, (picked, total) = refs[:n_row], refs[n_row:-2], refs[-2:]
    kmax = tiles_ref.shape[0]
    wide = total.shape[1]
    parts = BLK // part
    total[...] = jnp.zeros_like(total)
    places = []
    for i in range(kmax * parts):
        k, to = i // parts, pl.ds(i % parts * part, part)
        number = numbers_ref[0, i]
        source, row = number & (FIELD - 1), (number // FIELD) & (FIELD - 1)
        places.append(pl.ds(pl.multiple_of(number // (FIELD * FIELD) * part, part), part))
        block = pl.ds(pl.multiple_of(row * part, part), part)

        @pl.when(source == n_row)
        def _(k=k, to=to):
            picked[k, to, :] = jnp.zeros((part, wide), BF16)

        for p in range(n_row):
            columns = slice(at, at + wide) if p < 2 else slice(None)

            @pl.when(source == p)
            def _(k=k, to=to, p=p, block=block, columns=columns):
                picked[k, to, :] = pieces[p][block, columns]

    for k in range(kmax):
        product = jnp.dot(tiles_ref[k], picked[k], preferred_element_type=F32)
        for j in range(parts):
            total[places[k * parts + j], :] += product[j * part:(j + 1) * part, :]

    quarter = total.shape[0] // 4
    for q, out_ref in enumerate(out_refs):
        out_ref[...] = total[q * quarter:(q + 1) * quarter, :].astype(BF16)


def tile_products(numbers, tiles, pieces, at):
    n_row, n_col = lax.axis_size("row"), lax.axis_size("col")
    wide = pieces[-1].shape[1]
    quarter = jax.ShapeDtypeStruct((RBG * BLK // 4, wide), BF16)
    vmem = pl.BlockSpec(memory_space=pltpu.VMEM)
    return pl.pallas_call(
        functools.partial(tiles_kernel, at=at, n_row=n_row, part=min(BLK, pieces[0].shape[0], RBG * BLK // n_col)),
        out_shape=(quarter,) * 4,
        in_specs=[vmem] * (2 + n_row),
        out_specs=(vmem,) * 4,
        scratch_shapes=[
            pltpu.VMEM((tiles.shape[0], BLK, wide), BF16),
            pltpu.VMEM((RBG * BLK, wide), F32),
        ],
        compiler_params=pltpu.CompilerParams(vmem_limit_bytes=VMEM_LIMIT),
        cost_estimate=pl.CostEstimate(
            flops=2 * tiles.shape[0] * BLK * BLK * wide, bytes_accessed=6 * 1024 * 1024, transcendentals=0),
    )(numbers, tiles, *pieces)


def early_part(terms, weight, at, before):
    n, wide = terms[0].shape
    f = weight.shape[1]

    def kernel(weight_ref, *refs):
        *terms, agg_ref, pre_ref = refs
        if before is not None:
            before_ref, *terms = terms
        total = terms[0][...].astype(F32)
        for term in terms[1:]:
            total += term[...].astype(F32)
        agg_ref[...] = total.astype(BF16)
        share = jnp.dot(agg_ref[...], weight_ref[at:at + wide, :], preferred_element_type=F32)
        pre_ref[...] = share if before is None else before_ref[...] + share

    vmem = pl.BlockSpec(memory_space=pltpu.VMEM)
    inputs = (weight, *([] if before is None else [before]), *terms)
    return pl.pallas_call(
        kernel,
        out_shape=(jax.ShapeDtypeStruct((n, wide), BF16), jax.ShapeDtypeStruct((n, f), F32)),
        in_specs=[vmem] * len(inputs),
        out_specs=(vmem,) * 2,
        compiler_params=pltpu.CompilerParams(vmem_limit_bytes=VMEM_LIMIT),
        cost_estimate=pl.CostEstimate(flops=COST, bytes_accessed=4 * n * f, transcendentals=0),
    )(*inputs)


def vertex_kernel(weight_ref, cot_ref, pre_ref, *refs, n_row, n_early, scale):
    early, (*terms, out_ref, keep_ref, send_ref, output, grad, sem) = refs[:n_early], refs[n_early:]
    me_row = lax.axis_index("row")
    cut = grad.shape[0] - terms[0].shape[1]
    total = terms[0][...].astype(F32)
    for term in terms[1:]:
        total += term[...].astype(F32)
    last = total.astype(BF16)
    preact = pre_ref[...] + jnp.dot(last, weight_ref[cut:, :], preferred_element_type=F32)
    power = jnp.exp(jnp.minimum(preact, 0.0))
    positive = preact > 0
    output[...] = jnp.where(positive, preact, power - 1.0).astype(BF16)
    copy = pltpu.make_async_copy(output, out_ref, sem)
    copy.start()
    grad_pre = (cot_ref[...].astype(F32) * jnp.where(positive, 1.0, power)).astype(BF16)
    over_rows = (((0,), (0,)), ((), ()))
    at = 0
    for aggregated in [ref[...] for ref in early] + [last]:
        wide = aggregated.shape[1]
        grad[at:at + wide, :] = lax.dot_general(
            aggregated, grad_pre, over_rows, preferred_element_type=F32) * scale
        at += wide
    part = grad.shape[0] // n_row
    for k in range(n_row):
        rows = grad[pl.ds(pl.multiple_of((me_row ^ k) * part, part), part), :].astype(BF16)
        target = send_ref if k % 2 else keep_ref
        target[(k // 2) * part:(k // 2 + 1) * part, :] = rows
    copy.wait()


def vertex_step(weight, cotangent, pre, early, terms, scale):
    n_row = lax.axis_size("row")
    n, f = cotangent.shape
    half = jax.ShapeDtypeStruct((f // 2, f), BF16)
    vmem = pl.BlockSpec(memory_space=pltpu.VMEM)
    return pl.pallas_call(
        functools.partial(vertex_kernel, n_row=n_row, n_early=len(early), scale=scale),
        out_shape=(jax.ShapeDtypeStruct((n, f), BF16), half, half),
        in_specs=[vmem] * (3 + len(early) + len(terms)),
        out_specs=(pl.BlockSpec(memory_space=pl.ANY), vmem, vmem),
        scratch_shapes=[pltpu.VMEM((n, f), BF16), pltpu.VMEM((f, f), F32), pltpu.SemaphoreType.DMA],
        compiler_params=pltpu.CompilerParams(vmem_limit_bytes=VMEM_LIMIT),
        cost_estimate=pl.CostEstimate(
            flops=4 * n * f * f, bytes_accessed=4 * 1024 * 1024, transcendentals=n * f),
    )(weight, cotangent, pre, *early, *terms)


def join(pieces, core, whole=None):
    n = 2 * len(pieces)
    part, f = pieces[0].shape

    def kernel(*refs):
        *refs, out_ref, buffer, sems = refs
        me_row = lax.axis_index("row")
        copies = []
        for k, ref in enumerate(refs[:n // 2]):
            buffer[k] = ref[...].astype(F32)
            at = pl.multiple_of((me_row ^ (2 * k + core)) * part, part)
            copies.append(pltpu.make_async_copy(buffer.at[k], out_ref.at[pl.ds(at, part), :], sems.at[k]))
            copies[k].start()
        for copy in copies:
            copy.wait()

    vmem, any_space = pl.BlockSpec(memory_space=pltpu.VMEM), pl.BlockSpec(memory_space=pl.ANY)
    return pl.pallas_call(
        kernel,
        out_shape=jax.ShapeDtypeStruct((n * part, f), F32),
        in_specs=[vmem] * (n // 2) + ([] if whole is None else [any_space]),
        out_specs=any_space,
        scratch_shapes=[pltpu.VMEM((n // 2, part, f), F32), pltpu.SemaphoreType.DMA((n // 2,))],
        input_output_aliases={} if whole is None else {n // 2: 0},
        compiler_params=pltpu.CompilerParams(vmem_limit_bytes=VMEM_LIMIT),
    )(*pieces, *([] if whole is None else [whole]))


def reduce_gradient(keep, send):
    n_row, n_col = lax.axis_size("row"), lax.axis_size("col")
    part = keep.shape[0] // (n_row // 2)
    chip = keep.astype(F32) + swap(send, "row", 1).astype(F32)
    mine = chip[:part]
    for k in range(1, n_row // 2):
        mine = mine + swap(chip[k * part:(k + 1) * part].astype(BF16), "row", 2 * k).astype(F32)
    rounded, bit = mine.astype(BF16), 1
    while bit < n_col:
        if 2 * bit < n_col:
            others = [swap(rounded, "col", m * bit) for m in (1, 2, 3)]
            rounded = ((rounded.astype(F32) + others[0].astype(F32)) + (others[1].astype(F32) + others[2].astype(F32))).astype(BF16)
            bit *= 4
        else:
            rounded = plus(rounded, swap(rounded, "col", bit))
            bit *= 2
    even = [swap(rounded, "row", k) if k else rounded for k in range(0, n_row, 2)]
    odd = [swap(piece, "row", 1) for piece in even]
    return join(odd, 1, join(even, 0))


def plus(*terms):
    return sum((t.astype(F32) for t in terms[1:]), terms[0].astype(F32)).astype(BF16)


def finish(terms):
    n_col, bit = lax.axis_size("col"), 4
    while bit < n_col:
        mine = plus(*terms)
        half = mine.shape[0] // 2
        terms = mine[:half], swap(mine[half:], "col", bit)
        bit *= 2
    return terms


def hold(x):
    def kernel(x_ref, out_ref):
        out_ref[...] = x_ref[...]

    vmem = pl.BlockSpec(memory_space=pltpu.VMEM)
    return pl.pallas_call(
        kernel,
        out_shape=jax.ShapeDtypeStruct(x.shape, x.dtype),
        in_specs=[vmem],
        out_specs=vmem,
        compiler_params=pltpu.CompilerParams(vmem_limit_bytes=VMEM_LIMIT),
        cost_estimate=pl.CostEstimate(flops=COST, bytes_accessed=4 * x.size, transcendentals=0),
    )(x)


def local(features, tile_values, tile_index, tile_count, weight, cotangent):
    n_row, n_col = lax.axis_size("row"), lax.axis_size("col")
    starts = [sum(CHUNKS[:j]) for j in range(len(CHUNKS))]
    blocks, own, tiles, index, count = relay_chips(
        features[:, :CHUNKS[0]], features, tile_values[0, 0], tile_index[0, 0], tile_count[0, 0])
    numbers = slot_numbers(index, count, features.shape[0])
    tiles = stage(tiles)
    core = swap(own, "row", 1)
    keep, summed, pre = (), [], None
    for at, wide in zip(starts, CHUNKS):
        final = at + wide == features.shape[1]
        if at:
            early, *blocks = lax.optimization_barrier((features, *blocks))
            late, *keep = lax.optimization_barrier((features, *keep))
            blocks = gather_chips(early[:, at:at + wide], late[:, at:at + wide])
        pieces = [own, core]
        for block in blocks:
            pieces += [block, swap(block, "row", 1)]
        *keep, near, away = tile_products(numbers, tiles, pieces, at)
        if at:
            away, terms[0] = lax.optimization_barrier((away, hold(terms[0])))
        got = swap(away, "col", 1)
        send = plus(keep[1], got)
        if at:
            aggregated, pre = early_part(finish(terms), weight, done, pre)
            send, aggregated, pre = lax.optimization_barrier((send, aggregated, pre))
            summed.append(aggregated)
        near, got = lax.optimization_barrier((near, got))
        cut = near.shape[0] // (2 if final else 1)
        arrived = [swap(near[i:i + cut], "col", 1) for i in range(0, near.shape[0], cut)]
        terms, done = [keep[0], swap(send, "col", 2), jnp.concatenate(arrived)], at
    scale = 1.0 / math.sqrt(cotangent.shape[0] * n_row * n_col)
    output, grad_keep, grad_send = vertex_step(weight, cotangent, pre, summed, finish(terms), scale)
    return output, reduce_gradient(grad_keep, grad_send)


def solution(mesh):
    placed = (
        P(("col", "row"), None),
        P("row", "col", None, None, None),
        P("row", "col", None),
        P("row", "col"),
        P(),
        P(("row", "col"), None),
    )
    return jax.shard_map(
        local, mesh=mesh, in_specs=placed, out_specs=(P(("row", "col"), None), P()), check_vma=False
    )
```

```python
import functools
import math

import jax
import jax.numpy as jnp
from jax import lax
from jax.experimental import pallas as pl
from jax.experimental.pallas import tpu as pltpu
from jax.sharding import PartitionSpec as P

BLK = 256
RBG = 8
CHUNKS = (256, 256)
FIELD = 256
COST = 15 * 10**9
VMEM_LIMIT = 48 * 1024 * 1024
F32, BF16 = jnp.float32, jnp.bfloat16


def swap(x, axis, mask):
    return lax.ppermute(x, axis, [(i, i ^ mask) for i in range(lax.axis_size(axis))])


def bit_reversed(i, bits):
    out = 0 * i
    for b in range(bits):
        out = out + (((i >> b) & 1) << (bits - 1 - b))
    return out


def gather_chips(early, late):
    return [swap(early if k & (k - 1) == 0 else late, "row", k) for k in range(2, lax.axis_size("row"), 2)]


def relay_chips(x, *later):
    half = x.shape[0] // 2
    masks = sorted(range(2, lax.axis_size("row"), 2), key=lambda k: (bin(k).count("1"), k))
    near = [k for k in masks if k & (k - 1) == 0]
    halves = {}
    for early in (True, False):
        for k in near:
            h = int((k != near[0]) == early)
            halves[k, h] = swap(x[h * half:(h + 1) * half], "row", k)
    first = [(k, int(k != near[0])) for k in near]
    arrived, later = lax.optimization_barrier(([halves[key] for key in first], later))
    halves.update(zip(first, arrived))
    for k in masks[len(near):]:
        low, high = k & -k, 1 << (k.bit_length() - 1)
        halves[k, 0] = swap(halves[k ^ high, 0], "row", high)
        halves[k, 1] = swap(halves[k ^ low, 1], "row", low)
    return [jnp.concatenate([halves[k, 0], halves[k, 1]]) for k in sorted(masks)], *later


def stage(x):
    def kernel(x_ref, out_ref, sem):
        copy = pltpu.make_async_copy(x_ref, out_ref, sem)
        copy.start()
        copy.wait()

    return pl.pallas_call(
        kernel,
        out_shape=jax.ShapeDtypeStruct(x.shape, x.dtype),
        in_specs=[pl.BlockSpec(memory_space=pl.ANY)],
        out_specs=pl.BlockSpec(memory_space=pltpu.VMEM),
        scratch_shapes=[pltpu.SemaphoreType.DMA],
        compiler_params=pltpu.CompilerParams(vmem_limit_bytes=VMEM_LIMIT),
    )(x)


def slot_numbers(index, count, rows):
    n_row, n_col = lax.axis_size("row"), lax.axis_size("col")
    own = RBG * BLK // n_col
    part, bits = min(BLK, rows, own), n_col.bit_length() - 1
    col_groups = rows * n_row // BLK
    live = jnp.arange(index.shape[0]) < count
    along = jnp.arange(0, BLK, part)
    first = (index % col_groups * BLK)[:, None] + along
    source = jnp.where(live[:, None], (first // rows) ^ lax.axis_index("row"), n_row)
    target = (index // col_groups * BLK)[:, None] + along
    place = bit_reversed((target // own) ^ lax.axis_index("col"), bits) * own + target % own
    numbers = (source + FIELD * (first % rows // part) + FIELD * FIELD * (place // part)).reshape(-1)
    return jnp.broadcast_to(jnp.pad(numbers.astype(jnp.int32), (0, 128 - numbers.size)), (8, 128))


def tiles_kernel(numbers_ref, tiles_ref, *refs, at, n_row, part):
    pieces, out_refs, (picked, total) = refs[:n_row], refs[n_row:-2], refs[-2:]
    kmax = tiles_ref.shape[0]
    wide = total.shape[1]
    parts = BLK // part
    total[...] = jnp.zeros_like(total)
    places = []
    for i in range(kmax * parts):
        k, to = i // parts, pl.ds(i % parts * part, part)
        number = numbers_ref[0, i]
        source, row = number & (FIELD - 1), (number // FIELD) & (FIELD - 1)
        places.append(pl.ds(pl.multiple_of(number // (FIELD * FIELD) * part, part), part))
        block = pl.ds(pl.multiple_of(row * part, part), part)

        @pl.when(source == n_row)
        def _(k=k, to=to):
            picked[k, to, :] = jnp.zeros((part, wide), BF16)

        for p in range(n_row):
            columns = slice(at, at + wide) if p < 2 else slice(None)

            @pl.when(source == p)
            def _(k=k, to=to, p=p, block=block, columns=columns):
                picked[k, to, :] = pieces[p][block, columns]

    for k in range(kmax):
        product = jnp.dot(tiles_ref[k], picked[k], preferred_element_type=F32)
        for j in range(parts):
            total[places[k * parts + j], :] += product[j * part:(j + 1) * part, :]

    quarter = total.shape[0] // 4
    for q, out_ref in enumerate(out_refs):
        out_ref[...] = total[q * quarter:(q + 1) * quarter, :].astype(BF16)


def tile_products(numbers, tiles, pieces, at):
    n_row, n_col = lax.axis_size("row"), lax.axis_size("col")
    wide = pieces[-1].shape[1]
    quarter = jax.ShapeDtypeStruct((RBG * BLK // 4, wide), BF16)
    vmem = pl.BlockSpec(memory_space=pltpu.VMEM)
    return pl.pallas_call(
        functools.partial(tiles_kernel, at=at, n_row=n_row, part=min(BLK, pieces[0].shape[0], RBG * BLK // n_col)),
        out_shape=(quarter,) * 4,
        in_specs=[vmem] * (2 + n_row),
        out_specs=(vmem,) * 4,
        scratch_shapes=[
            pltpu.VMEM((tiles.shape[0], BLK, wide), BF16),
            pltpu.VMEM((RBG * BLK, wide), F32),
        ],
        compiler_params=pltpu.CompilerParams(vmem_limit_bytes=VMEM_LIMIT),
        cost_estimate=pl.CostEstimate(
            flops=2 * tiles.shape[0] * BLK * BLK * wide, bytes_accessed=6 * 1024 * 1024, transcendentals=0),
    )(numbers, tiles, *pieces)


def early_part(terms, weight, at, before):
    n, wide = terms[0].shape
    f = weight.shape[1]

    def kernel(weight_ref, *refs):
        *terms, agg_ref, pre_ref = refs
        if before is not None:
            before_ref, *terms = terms
        total = terms[0][...].astype(F32)
        for term in terms[1:]:
            total += term[...].astype(F32)
        agg_ref[...] = total.astype(BF16)
        share = jnp.dot(agg_ref[...], weight_ref[at:at + wide, :], preferred_element_type=F32)
        pre_ref[...] = share if before is None else before_ref[...] + share

    vmem = pl.BlockSpec(memory_space=pltpu.VMEM)
    inputs = (weight, *([] if before is None else [before]), *terms)
    return pl.pallas_call(
        kernel,
        out_shape=(jax.ShapeDtypeStruct((n, wide), BF16), jax.ShapeDtypeStruct((n, f), F32)),
        in_specs=[vmem] * len(inputs),
        out_specs=(vmem,) * 2,
        compiler_params=pltpu.CompilerParams(vmem_limit_bytes=VMEM_LIMIT),
        cost_estimate=pl.CostEstimate(flops=COST, bytes_accessed=4 * n * f, transcendentals=0),
    )(*inputs)


def vertex_kernel(weight_ref, cot_ref, pre_ref, *refs, n_row, n_early, scale):
    early, (*terms, out_ref, keep_ref, send_ref, output, grad, sem) = refs[:n_early], refs[n_early:]
    me_row = lax.axis_index("row")
    cut = grad.shape[0] - terms[0].shape[1]
    total = terms[0][...].astype(F32)
    for term in terms[1:]:
        total += term[...].astype(F32)
    last = total.astype(BF16)
    preact = pre_ref[...] + jnp.dot(last, weight_ref[cut:, :], preferred_element_type=F32)
    power = jnp.exp(jnp.minimum(preact, 0.0))
    positive = preact > 0
    output[...] = jnp.where(positive, preact, power - 1.0).astype(BF16)
    copy = pltpu.make_async_copy(output, out_ref, sem)
    copy.start()
    grad_pre = (cot_ref[...].astype(F32) * jnp.where(positive, 1.0, power)).astype(BF16)
    over_rows = (((0,), (0,)), ((), ()))
    at = 0
    for aggregated in [ref[...] for ref in early] + [last]:
        wide = aggregated.shape[1]
        grad[at:at + wide, :] = lax.dot_general(
            aggregated, grad_pre, over_rows, preferred_element_type=F32) * scale
        at += wide
    part = grad.shape[0] // n_row
    for k in range(n_row):
        rows = grad[pl.ds(pl.multiple_of((me_row ^ k) * part, part), part), :].astype(BF16)
        target = send_ref if k % 2 else keep_ref
        target[(k // 2) * part:(k // 2 + 1) * part, :] = rows
    copy.wait()


def vertex_step(weight, cotangent, pre, early, terms, scale):
    n_row = lax.axis_size("row")
    n, f = cotangent.shape
    half = jax.ShapeDtypeStruct((f // 2, f), BF16)
    vmem = pl.BlockSpec(memory_space=pltpu.VMEM)
    return pl.pallas_call(
        functools.partial(vertex_kernel, n_row=n_row, n_early=len(early), scale=scale),
        out_shape=(jax.ShapeDtypeStruct((n, f), BF16), half, half),
        in_specs=[vmem] * (3 + len(early) + len(terms)),
        out_specs=(pl.BlockSpec(memory_space=pl.ANY), vmem, vmem),
        scratch_shapes=[pltpu.VMEM((n, f), BF16), pltpu.VMEM((f, f), F32), pltpu.SemaphoreType.DMA],
        compiler_params=pltpu.CompilerParams(vmem_limit_bytes=VMEM_LIMIT),
        cost_estimate=pl.CostEstimate(
            flops=4 * n * f * f, bytes_accessed=4 * 1024 * 1024, transcendentals=n * f),
    )(weight, cotangent, pre, *early, *terms)


def join(pieces, core, whole=None):
    n = 2 * len(pieces)
    part, f = pieces[0].shape

    def kernel(*refs):
        *refs, out_ref, buffer, sems = refs
        me_row = lax.axis_index("row")
        copies = []
        for k, ref in enumerate(refs[:n // 2]):
            buffer[k] = ref[...].astype(F32)
            at = pl.multiple_of((me_row ^ (2 * k + core)) * part, part)
            copies.append(pltpu.make_async_copy(buffer.at[k], out_ref.at[pl.ds(at, part), :], sems.at[k]))
            copies[k].start()
        for copy in copies:
            copy.wait()

    vmem, any_space = pl.BlockSpec(memory_space=pltpu.VMEM), pl.BlockSpec(memory_space=pl.ANY)
    return pl.pallas_call(
        kernel,
        out_shape=jax.ShapeDtypeStruct((n * part, f), F32),
        in_specs=[vmem] * (n // 2) + ([] if whole is None else [any_space]),
        out_specs=any_space,
        scratch_shapes=[pltpu.VMEM((n // 2, part, f), F32), pltpu.SemaphoreType.DMA((n // 2,))],
        input_output_aliases={} if whole is None else {n // 2: 0},
        compiler_params=pltpu.CompilerParams(vmem_limit_bytes=VMEM_LIMIT),
    )(*pieces, *([] if whole is None else [whole]))


def reduce_gradient(keep, send):
    n_row, n_col = lax.axis_size("row"), lax.axis_size("col")
    part = keep.shape[0] // (n_row // 2)
    chip = keep.astype(F32) + swap(send, "row", 1).astype(F32)
    mine = chip[:part]
    for k in range(1, n_row // 2):
        mine = mine + swap(chip[k * part:(k + 1) * part].astype(BF16), "row", 2 * k).astype(F32)
    rounded, bit = mine.astype(BF16), 1
    while bit < n_col:
        if 2 * bit < n_col:
            others = [swap(rounded, "col", m * bit) for m in (1, 2, 3)]
            rounded = ((rounded.astype(F32) + others[0].astype(F32)) + (others[1].astype(F32) + others[2].astype(F32))).astype(BF16)
            bit *= 4
        else:
            rounded = plus(rounded, swap(rounded, "col", bit))
            bit *= 2
    even = [swap(rounded, "row", k) if k else rounded for k in range(0, n_row, 2)]
    odd = [swap(piece, "row", 1) for piece in even]
    return join(odd, 1, join(even, 0))


def plus(*terms):
    return sum((t.astype(F32) for t in terms[1:]), terms[0].astype(F32)).astype(BF16)


def finish(terms):
    n_col, bit = lax.axis_size("col"), 4
    while bit < n_col:
        mine = plus(*terms)
        half = mine.shape[0] // 2
        terms = mine[:half], swap(mine[half:], "col", bit)
        bit *= 2
    return terms


def hold(x):
    def kernel(x_ref, out_ref):
        out_ref[...] = x_ref[...]

    vmem = pl.BlockSpec(memory_space=pltpu.VMEM)
    return pl.pallas_call(
        kernel,
        out_shape=jax.ShapeDtypeStruct(x.shape, x.dtype),
        in_specs=[vmem],
        out_specs=vmem,
        compiler_params=pltpu.CompilerParams(vmem_limit_bytes=VMEM_LIMIT),
        cost_estimate=pl.CostEstimate(flops=COST, bytes_accessed=4 * x.size, transcendentals=0),
    )(x)


def local(features, tile_values, tile_index, tile_count, weight, cotangent):
    n_row, n_col = lax.axis_size("row"), lax.axis_size("col")
    starts = [sum(CHUNKS[:j]) for j in range(len(CHUNKS))]
    blocks, own, tiles, index, count = relay_chips(
        features[:, :CHUNKS[0]], features, tile_values[0, 0], tile_index[0, 0], tile_count[0, 0])
    numbers = slot_numbers(index, count, features.shape[0])
    tiles = stage(tiles)
    core = swap(own, "row", 1)
    keep, summed, pre = (), [], None
    for at, wide in zip(starts, CHUNKS):
        final = at + wide == features.shape[1]
        if at:
            early, blocks[0] = lax.optimization_barrier((features, blocks[0]))
            late, *keep = lax.optimization_barrier((features, *keep))
            blocks = gather_chips(early[:, at:at + wide], late[:, at:at + wide])
        pieces = [own, core]
        for block in blocks:
            pieces += [block, swap(block, "row", 1)]
        *keep, near, away = tile_products(numbers, tiles, pieces, at)
        if at:
            away, terms[0] = lax.optimization_barrier((away, hold(terms[0])))
        got = swap(away, "col", 1)
        send = plus(keep[1], got)
        if at:
            aggregated, pre = early_part(finish(terms), weight, done, pre)
            send, aggregated, pre = lax.optimization_barrier((send, aggregated, pre))
            summed.append(aggregated)
        near, got = lax.optimization_barrier((near, got))
        cut = near.shape[0] // (4 if final else 1)
        arrived = [swap(near[i:i + cut], "col", 1) for i in range(0, near.shape[0], cut)]
        terms, done = [keep[0], swap(send, "col", 2), jnp.concatenate(arrived)], at
    scale = 1.0 / math.sqrt(cotangent.shape[0] * n_row * n_col)
    output, grad_keep, grad_send = vertex_step(weight, cotangent, pre, summed, finish(terms), scale)
    return output, reduce_gradient(grad_keep, grad_send)


def solution(mesh):
    placed = (
        P(("col", "row"), None),
        P("row", "col", None, None, None),
        P("row", "col", None),
        P("row", "col"),
        P(),
        P(("row", "col"), None),
    )
    return jax.shard_map(
        local, mesh=mesh, in_specs=placed, out_specs=(P(("row", "col"), None), P()), check_vma=False
    )
```
